32 devices in a mesh: cluster: 4 (over x, core), blk: 8 (over z, y).
Axes of the slice: x: 2, y: 2, z: 4, core: 2. Of those that a mesh axis runs over, the one named last changes fastest.
Arguments:
- tokens: bfloat16 [6144, 2048], P(('cluster', 'blk')), may hold values from -40 to 40
- w_query: bfloat16 [2048, 2048], replicated, may hold values from -0.21875 to 0.21875
- w_key: bfloat16 [2048, 2048], replicated, may hold values from -0.21875 to 0.21875
- w_value: bfloat16 [2048, 2048], replicated, may hold values from -0.125 to 0.125
- cluster_ids: int32 [6144, 1], P(('cluster', 'blk')), may hold values from 0 to 3; in each aligned block of 192 rows (0 to 191, 192 to 383, ...) at most 64 rows name the same one
Outputs:
- attended: bfloat16 [6144, 2048], P(('cluster', 'blk'))
The draws below stay inside these ranges and needn't reach their ends.
Inputs may be any that keep to these rules, and one draw needn't show every extreme that they name: `cluster_ids`: among the 192 tokens of one device no cluster appears more than 64 times; some device holds exactly 64 of some cluster; every cluster has tokens.
All inputs are finite; a program needn't handle non-finite values.
Results may differ from the reference program's by a relative error of at most 0.0045.
The reference program's roundings to bfloat16 on the way count: a program that leaves them out, or rounds other values in their place, can miss the bound.
Values may be sent and summed in bfloat16 or wider, within the bound.
A program may use at most 192 MiB of HBM per device.

```python
import math
import jax
import jax.numpy as jnp
import numpy as np
from jax import lax

D = 2048
HEADS = 16
HEAD_DIM = 128
TOK_DEV = 192
CLUSTERS = 4
SLOT = 64
TOKENS = 6144
N_BLK = 8


def draw_tokens(key, part):
    first = jax.random.fold_in(key, 0)
    normal_part = jax.random.normal(first, (TOKENS, D), jnp.float32)
    values = normal_part
    return jnp.clip(values, -40.0, 40.0).astype(jnp.bfloat16)


def assign_block(stream_key, own, number, rows, count, top, most, slope):
    sequence = jax.random.permutation(stream_key, count)
    packed, usual = portions_of(count, rows * top, most, slope, True), portions_of(count, rows * top, most, slope, False)
    places = jnp.arange(count)

    def named(sizes, offset_by):
        used = int((sizes > 0).sum())
        fixed = max(1, used // 4)
        shifted = fixed + (places - fixed + offset_by * (used - fixed)) % max(1, count - fixed)
        return jnp.zeros((count,), jnp.int32).at[sequence[jnp.where(places < fixed, places, shifted)]].set(jnp.asarray(sizes, jnp.int32))

    sizes = jnp.where(number % 4 == 0, named(packed, number // 4), named(usual, number - number // 4 - 1))
    mixed = jax.random.permutation(jax.random.fold_in(own, 3), count)
    source_of, receiver = mixed[0:count // 2 * 2:2], mixed[1:count // 2 * 2:2]
    margin = jnp.minimum(sizes[source_of] - 1, most - sizes[receiver]) // 2
    margin = jnp.where((source_of == sequence[0]) | (receiver == sequence[0]) | (sizes[receiver] == 0), 0, jnp.maximum(margin, 0))
    shifted = jax.random.randint(jax.random.fold_in(own, 4), (count // 2,), 0, 1 << 20) % (margin + 1)
    sizes = sizes.at[source_of].add(-shifted).at[receiver].add(shifted)
    members = jnp.searchsorted(jnp.cumsum(sizes), jnp.arange(rows * top), side="right").astype(jnp.int32)
    listing = members.reshape(top, rows).T
    listing = listing[jax.random.permutation(jax.random.fold_in(own, 1), rows)]
    offset_by = jax.random.randint(jax.random.fold_in(own, 2), (rows, 1), 0, top)
    return jnp.take_along_axis(listing, (jnp.arange(top)[None, :] + offset_by) % top, axis=1)


def portions_of(count, total, reach, skew, full):
    portions = [(1 << 20) // math.isqrt(rank ** skew) + 1 for rank in range(1, count + 1)]
    largest = reach if full else min(reach, max(-(-total // count), total * portions[0] // sum(portions)))
    least = 1 if total - largest >= count - 1 else 0
    holding, surplus = [largest] + [least] * (count - 1), total - largest - least * (count - 1)
    while surplus > 0:
        candidates = [i for i in range(1, count) if holding[i] < largest] or [i for i in range(1, count) if holding[i] < reach]
        pool, remaining = sum([portions[i] for i in candidates]), surplus
        for i in candidates:
            addition = min(reach - holding[i], max(1, remaining * portions[i] // pool), surplus)
            holding[i] = holding[i] + addition
            surplus = surplus - addition
    return np.array(holding)


def scatter_about(own_key, shape, scale, limit, held_as=jnp.bfloat16):
    values = scale * jax.random.normal(own_key, shape, jnp.float32)
    return jnp.clip(values, min=-limit, max=limit).astype(held_as)


def setup_inputs(seed: int = 0) -> dict:
    key_of = jax.random.split(jax.random.key(seed), 6)
    tokens = draw_tokens(jax.random.fold_in(key_of[5], 71), 0)
    w_query = scatter_about(key_of[1], (D, D), (2 * D // 5) ** -0.5, 0.21875)
    w_key = scatter_about(key_of[2], (D, D), (2 * D // 5) ** -0.5, 0.21875)
    w_value = scatter_about(key_of[3], (D, D), D ** -0.5, 0.125)
    cluster_ids_keys = jax.random.split(jax.random.fold_in(key_of[4], 1), TOKENS // TOK_DEV)
    cluster_ids_turns = jax.random.permutation(jax.random.fold_in(key_of[4], 3), TOKENS // TOK_DEV)
    cluster_ids = jax.vmap(lambda own, number: assign_block(jax.random.fold_in(key_of[4], 2), own, number, TOK_DEV, CLUSTERS, 1, SLOT, 2))(cluster_ids_keys, cluster_ids_turns).reshape((TOKENS, 1))
    return {"tokens": tokens, "w_query": w_query, "w_key": w_key, "w_value": w_value, "cluster_ids": cluster_ids}


MASKED_SCORE = -1e30


def one_head(operands):
    head_query, head_key, head_value, live_keys = operands
    scores = jnp.dot(head_query, head_key.T, preferred_element_type=jnp.float32) * (HEAD_DIM ** -0.5)
    scores = jnp.where(live_keys[None, :], scores, MASKED_SCORE)
    row_max = jnp.max(scores, axis=1, keepdims=True)
    softmax_w = jnp.where(live_keys[None, :], jnp.exp(scores - row_max), 0.0)
    row_sum = jnp.sum(softmax_w, axis=1)
    numerator = jnp.dot(softmax_w.astype(jnp.bfloat16), head_value, preferred_element_type=jnp.float32)
    return numerator / row_sum[:, None]


def reference(tokens, w_query, w_key, w_value, cluster_ids):
    labels = cluster_ids[:, 0].astype(jnp.int32)
    query = jnp.dot(tokens, w_query, preferred_element_type=jnp.float32).astype(jnp.bfloat16)
    keys_all = jnp.dot(tokens, w_key, preferred_element_type=jnp.float32).astype(jnp.bfloat16)
    values_all = jnp.dot(tokens, w_value, preferred_element_type=jnp.float32).astype(jnp.bfloat16)
    order = jnp.argsort(labels, stable=True).astype(jnp.int32)
    onehot = (labels[:, None] == jnp.arange(CLUSTERS, dtype=jnp.int32)[None, :]).astype(jnp.int32)
    counts = jnp.sum(onehot, axis=0).astype(jnp.int32)
    starts = (jnp.cumsum(counts) - counts).astype(jnp.int32)
    most_rows = CLUSTERS * N_BLK * SLOT

    def per_cluster(which):
        positions = starts[which] + jnp.arange(most_rows, dtype=jnp.int32)
        live_rows = jnp.arange(most_rows, dtype=jnp.int32) < counts[which]
        member = order[jnp.minimum(positions, TOKENS - 1)].astype(jnp.int32)
        heads_query = query[member].reshape(most_rows, HEADS, HEAD_DIM).transpose(1, 0, 2)
        heads_key = keys_all[member].reshape(most_rows, HEADS, HEAD_DIM).transpose(1, 0, 2)
        heads_value = values_all[member].reshape(most_rows, HEADS, HEAD_DIM).transpose(1, 0, 2)
        live_heads = jnp.broadcast_to(live_rows[None, :], (HEADS, most_rows))
        outputs = lax.map(one_head, (heads_query, heads_key, heads_value, live_heads))
        out_rows = outputs.transpose(1, 0, 2).reshape(most_rows, D).astype(jnp.bfloat16)
        targets = jnp.where(live_rows, member, TOKENS).astype(jnp.int32)
        return out_rows, targets

    out_rows, targets = lax.map(per_cluster, jnp.arange(CLUSTERS, dtype=jnp.int32))
    result = jnp.zeros((TOKENS, D), jnp.bfloat16)
    return result.at[targets.reshape(-1)].set(out_rows.reshape(-1, D), mode="drop")
```

```python
import functools

import jax
import jax.numpy as jnp
from jax import lax
from jax.experimental import pallas as pl
from jax.experimental.pallas import tpu as pltpu
from jax.sharding import PartitionSpec as P

HEADS = 16
MASKED_SCORE = -1e30
LOG2E = 1.4426950408889634
PAIR = 2
GROUP = 4
MESH = pl.DeviceIdType.MESH


def kernel(groups, blks, parts, cap, tok_ref, wq_ref, wk_ref, wv_ref, lrow_ref, lcol_ref, out_ref,
           w_buf, kv_out, q_out, ids_out, kv_all, q_in, ids_all, k_slots, v_slots, q_slots, att_slots,
           ret_out, gathered, w_sem, kv_ss, kv_rs, q_ss, q_rs, id_ss, id_rs, fkv_ss, fkv_rs, fid_ss,
           fid_rs, ret_ss, ret_rs, own_sem):
    rows, width = tok_ref.shape
    size = width // HEADS
    slots = groups * cap
    pairs = HEADS // PAIR
    pw = PAIR * size
    ci, bi = lax.axis_index("cluster"), lax.axis_index("blk")
    part = lax.rem(ci, parts)
    me = (ci // parts) * blks + bi
    own_pair = me // PAIR

    def holder(head, its_part):
        return {"cluster": (head // blks) * parts + its_part, "blk": lax.rem(head, blks)}

    def pair_out(t):
        return lax.rem(own_pair + t, pairs)

    def source_at(i):
        return lax.rem(own_pair + pairs - i // PAIR, pairs) * PAIR + lax.rem(i, PAIR)

    def w_copies(t, slot):
        cols = pl.ds(pl.multiple_of(pair_out(t) * pw, pw), pw)
        return [
            pltpu.make_async_copy(ref.at[:, cols], w_buf.at[slot, :, pl.ds(n * pw, pw)], w_sem.at[slot, n])
            for n, ref in enumerate((wq_ref, wk_ref, wv_ref))
        ]

    for copy in w_copies(0, 0):
        copy.start()

    barrier = pltpu.get_barrier_semaphore()

    @pl.loop(0, HEADS)
    def _(h):
        @pl.when(h != me)
        def _():
            pl.semaphore_signal(barrier, inc=1, device_id=holder(h, part), device_id_type=MESH)

    for d in range(1, parts):
        pl.semaphore_signal(
            barrier, inc=1, device_id=holder(me, lax.rem(part + d, parts)), device_id_type=MESH
        )

    lab = lrow_ref[...]
    padded = lab.shape[1]
    earlier = (lcol_ref[...] == lab) & (
        lax.broadcasted_iota(jnp.int32, (rows, padded), 0)
        < lax.broadcasted_iota(jnp.int32, (rows, padded), 1)
    )
    rank = jnp.sum(earlier.astype(jnp.int32), axis=0, keepdims=True)
    target = jnp.where(lab >= 0, lab * cap + rank, -1)
    ids_out[...] = target
    ids_all[part, me] = target
    unit = (lax.broadcasted_iota(jnp.int32, (GROUP * cap, size), 1) == 0).astype(jnp.bfloat16)
    for c in range(groups):
        q_slots[c, :, size:] = unit

    pl.semaphore_wait(barrier, HEADS - 1 + parts - 1)

    def id_copy(h):
        return pltpu.make_async_remote_copy(
            ids_out, ids_all.at[part, me], id_ss.at[h], id_rs.at[me],
            device_id=holder(h, part), device_id_type=MESH)

    def kv_copy(h):
        return pltpu.make_async_remote_copy(
            kv_out.at[h], kv_all.at[part, me], kv_ss.at[h], kv_rs.at[me],
            device_id=holder(h, part), device_id_type=MESH)

    def q_copy(h):
        return pltpu.make_async_remote_copy(
            q_out.at[h], q_in.at[me], q_ss.at[h], q_rs.at[me],
            device_id=holder(h, part), device_id_type=MESH)

    def ret_copy(s):
        return pltpu.make_async_remote_copy(
            ret_out.at[s], gathered.at[:, pl.ds(pl.multiple_of(me * size, size), size)],
            ret_ss.at[s], ret_rs.at[me], device_id=holder(s, part), device_id_type=MESH)

    def kv_fwd(s, d):
        return pltpu.make_async_remote_copy(
            kv_all.at[part, s], kv_all.at[part, s], fkv_ss.at[d - 1, s], fkv_rs.at[d - 1, s],
            device_id=holder(me, lax.rem(part + d, parts)), device_id_type=MESH)

    def id_fwd(s, d):
        return pltpu.make_async_remote_copy(
            ids_all.at[part, s], ids_all.at[part, s], fid_ss.at[d - 1, s], fid_rs.at[d - 1, s],
            device_id=holder(me, lax.rem(part + d, parts)), device_id_type=MESH)

    @pl.loop(0, HEADS)
    def _(h):
        @pl.when(h != me)
        def _():
            id_copy(h).start()

    @pl.loop(0, pairs)
    def _(t):
        slot = lax.rem(t, 2)

        @pl.when(t + 1 < pairs)
        def _():
            for copy in w_copies(t + 1, 1 - slot):
                copy.start()

        for copy in w_copies(t, slot):
            copy.wait()
        made = jnp.dot(tok_ref[...], w_buf[slot], preferred_element_type=jnp.float32).astype(jnp.bfloat16)
        for j in range(PAIR):
            h = pair_out(t) * PAIR + j
            q = made[:, j * size:(j + 1) * size]
            k = made[:, pw + j * size:pw + (j + 1) * size]
            v = made[:, 2 * pw + j * size:2 * pw + (j + 1) * size]

            @pl.when(h != me)
            def _():
                kv_out[h, :, :size] = k
                kv_out[h, :, size:] = v
                q_out[h] = q
                kv_copy(h).start()

            @pl.when(h == me)
            def _():
                kv_all[part, me, :, :size] = k
                kv_all[part, me, :, size:] = v
                q_in[me] = q

    @pl.loop(0, HEADS)
    def _(i):
        h = lax.rem(own_pair * PAIR + i, HEADS)

        @pl.when(h != me)
        def _():
            q_copy(h).start()

    def spread(its_part, s):
        where = ids_all[its_part, s][:, :rows]
        return lax.broadcasted_iota(jnp.int32, (slots, rows), 0) == where

    def place_kv(its_part, s):
        hot = spread(its_part, s)
        placed = jnp.dot(
            hot.astype(jnp.bfloat16), kv_all[its_part, s], preferred_element_type=jnp.float32
        ).astype(jnp.bfloat16)
        live = jnp.sum(hot.astype(jnp.float32), axis=1, keepdims=True)
        bias = jnp.broadcast_to(jnp.where(live > 0, 0.0, MASKED_SCORE), (slots, size)).astype(jnp.bfloat16)
        at = pl.ds(pl.multiple_of((its_part * HEADS + s) * cap, cap), cap)
        for c in range(groups):
            mine = slice(c * cap, (c + 1) * cap)
            k_slots[c, at, :size] = placed[mine, :size]
            k_slots[c, at, size:] = bias[mine]
            v_slots[c, at, :] = placed[mine, size:]

    @pl.loop(0, HEADS)
    def _(i):
        s = source_at(i)

        @pl.when(s != me)
        def _():
            pltpu.make_async_remote_copy(
                ids_out, ids_all.at[part, s], id_ss.at[s], id_rs.at[s],
                device_id=holder(s, part), device_id_type=MESH).wait_recv()
            pltpu.make_async_remote_copy(
                kv_out.at[s], kv_all.at[part, s], kv_ss.at[s], kv_rs.at[s],
                device_id=holder(s, part), device_id_type=MESH).wait_recv()

        for d in range(1, parts):
            id_fwd(s, d).start()
            kv_fwd(s, d).start()
        place_kv(part, s)

    for d in range(1, parts):
        frm = lax.rem(part + parts - d, parts)

        @pl.loop(0, HEADS)
        def _(i):
            s = source_at(i)
            pltpu.make_async_remote_copy(
                ids_all.at[frm, s], ids_all.at[frm, s], fid_ss.at[d - 1, s], fid_rs.at[d - 1, s],
                device_id=holder(me, frm), device_id_type=MESH).wait_recv()
            pltpu.make_async_remote_copy(
                kv_all.at[frm, s], kv_all.at[frm, s], fkv_ss.at[d - 1, s], fkv_rs.at[d - 1, s],
                device_id=holder(me, frm), device_id_type=MESH).wait_recv()
            place_kv(frm, s)

    factor = LOG2E * size ** (-0.5)

    @pl.loop(0, HEADS // GROUP)
    def _(g):
        for n in range(GROUP):
            s = source_at(g * GROUP + n)

            @pl.when(s != me)
            def _():
                pltpu.make_async_remote_copy(
                    q_out.at[s], q_in.at[s], q_ss.at[s], q_rs.at[s],
                    device_id=holder(s, part), device_id_type=MESH).wait_recv()

            placed = jnp.dot(
                spread(part, s).astype(jnp.bfloat16), q_in[s], preferred_element_type=jnp.float32
            ).astype(jnp.bfloat16)
            for c in range(groups):
                q_slots[c, n * cap:(n + 1) * cap, :size] = placed[c * cap:(c + 1) * cap]

        @pl.loop(0, groups)
        def _(c):
            scores = lax.dot_general(
                q_slots[c], k_slots[c], (((1,), (1,)), ((), ())), preferred_element_type=jnp.float32
            )
            top = jnp.max(scores, axis=1, keepdims=True)
            weights = jnp.exp2((scores - top) * factor)
            total = jnp.sum(weights, axis=1, keepdims=True)
            summed = jnp.dot(
                weights.astype(jnp.bfloat16), v_slots[c], preferred_element_type=jnp.float32
            )
            att_slots[c] = (summed / total).astype(jnp.bfloat16)

        for n in range(GROUP):
            s = source_at(g * GROUP + n)
            mine = jnp.concatenate(
                [att_slots[c, n * cap:(n + 1) * cap, :] for c in range(groups)], axis=0
            )
            back = lax.dot_general(
                spread(part, s).astype(jnp.bfloat16), mine, (((0,), (0,)), ((), ())),
                preferred_element_type=jnp.float32,
            ).astype(jnp.bfloat16)
            ret_out[s] = back

            @pl.when(s != me)
            def _():
                ret_copy(s).start()

            @pl.when(s == me)
            def _():
                own = pltpu.make_async_copy(
                    ret_out.at[s], gathered.at[:, pl.ds(pl.multiple_of(me * size, size), size)], own_sem)
                own.start()
                own.wait()

    @pl.loop(0, HEADS)
    def _(h):
        @pl.when(h != me)
        def _():
            id_copy(h).wait_send()
            kv_copy(h).wait_send()
            q_copy(h).wait_send()
            ret_copy(h).wait_send()
            pltpu.make_async_remote_copy(
                ret_out.at[h], gathered.at[:, pl.ds(pl.multiple_of(h * size, size), size)],
                ret_ss.at[h], ret_rs.at[h], device_id=holder(h, part), device_id_type=MESH).wait_recv()

        for d in range(1, parts):
            id_fwd(h, d).wait_send()
            kv_fwd(h, d).wait_send()

    out_ref[...] = gathered[...]


def per_device(tokens, w_query, w_key, w_value, cluster_ids):
    groups, blks = lax.axis_size("cluster"), lax.axis_size("blk")
    rows, width = tokens.shape
    size = width // HEADS
    parts = groups * blks // HEADS
    cap = 4 * rows // (3 * groups)
    padded = -(-rows // 128) * 128
    lab_row = jnp.pad(cluster_ids.reshape(1, rows), ((0, 0), (0, padded - rows)), constant_values=-1)
    vmem = pl.BlockSpec(memory_space=pltpu.VMEM)
    hbm = pl.BlockSpec(memory_space=pl.ANY)
    bf16 = jnp.bfloat16
    sem = pltpu.SemaphoreType.DMA
    others = max(parts - 1, 1)
    keys = parts * HEADS * cap
    return pl.pallas_call(
        functools.partial(kernel, groups, blks, parts, cap),
        out_shape=jax.ShapeDtypeStruct((rows, width), bf16),
        in_specs=[vmem, hbm, hbm, hbm, vmem, vmem],
        out_specs=vmem,
        scratch_shapes=[
            pltpu.VMEM((2, width, 3 * PAIR * size), bf16),
            pltpu.VMEM((HEADS, rows, 2 * size), bf16),
            pltpu.VMEM((HEADS, rows, size), bf16),
            pltpu.VMEM((1, padded), jnp.int32),
            pltpu.VMEM((parts, HEADS, rows, 2 * size), bf16),
            pltpu.VMEM((HEADS, rows, size), bf16),
            pltpu.VMEM((parts, HEADS, 1, padded), jnp.int32),
            pltpu.VMEM((groups, keys, 2 * size), bf16),
            pltpu.VMEM((groups, keys, size), bf16),
            pltpu.VMEM((groups, GROUP * cap, 2 * size), bf16),
            pltpu.VMEM((groups, GROUP * cap, size), bf16),
            pltpu.VMEM((HEADS, rows, size), bf16),
            pltpu.VMEM((rows, width), bf16),
            sem((2, 3)),
            sem((HEADS,)), sem((HEADS,)), sem((HEADS,)), sem((HEADS,)), sem((HEADS,)), sem((HEADS,)),
            sem((others, HEADS)), sem((others, HEADS)), sem((others, HEADS)), sem((others, HEADS)),
            sem((HEADS,)), sem((HEADS,)),
            sem,
        ],
        compiler_params=pltpu.CompilerParams(
            collective_id=0, has_side_effects=True, vmem_limit_bytes=60 * 1024 * 1024
        ),
    )(tokens, w_query, w_key, w_value, lab_row, cluster_ids)


def solution(mesh):
    return jax.shard_map(
        per_device,
        mesh=mesh,
        in_specs=(P(("cluster", "blk"), None), P(), P(), P(), P(("cluster", "blk"), None)),
        out_specs=P(("cluster", "blk"), None),
        check_vma=False,
    )
```

```python
import functools

import jax
import jax.numpy as jnp
from jax import lax
from jax.experimental import pallas as pl
from jax.experimental.pallas import tpu as pltpu
from jax.sharding import PartitionSpec as P

HEADS = 16
MASKED_SCORE = -1e30
LOG2E = 1.4426950408889634
PAIR = 2
GROUP = 4
MESH = pl.DeviceIdType.MESH


def kernel(groups, blks, parts, cap, tok_ref, wq_ref, wk_ref, wv_ref, lcol_ref, out_ref,
           w_buf, kv_out, q_out, ids_out, kv_all, q_in, ids_all, k_slots, v_slots, q_slots, att_slots,
           ret_out, gathered, w_sem, kv_ss, kv_rs, q_ss, q_rs, id_ss, id_rs, fkv_ss, fkv_rs, fid_ss,
           fid_rs, ret_ss, ret_rs, own_sem):
    rows, width = tok_ref.shape
    size = width // HEADS
    slots = groups * cap
    pairs = HEADS // PAIR
    pw = PAIR * size
    ci, bi = lax.axis_index("cluster"), lax.axis_index("blk")
    part = lax.rem(ci, parts)
    me = (ci // parts) * blks + bi
    own_pair = me // PAIR

    def holder(head, its_part):
        return {"cluster": (head // blks) * parts + its_part, "blk": lax.rem(head, blks)}

    def pair_out(t):
        return lax.rem(own_pair + t, pairs)

    def source_at(i):
        return lax.rem(own_pair + pairs - i // PAIR, pairs) * PAIR + lax.rem(i, PAIR)

    def w_copies(t, slot):
        cols = pl.ds(pl.multiple_of(pair_out(t) * pw, pw), pw)
        return [
            pltpu.make_async_copy(ref.at[:, cols], w_buf.at[slot, :, pl.ds(n * pw, pw)], w_sem.at[slot, n])
            for n, ref in enumerate((wq_ref, wk_ref, wv_ref))
        ]

    for copy in w_copies(0, 0):
        copy.start()

    barrier = pltpu.get_barrier_semaphore()

    @pl.loop(0, HEADS)
    def _(h):
        @pl.when(h != me)
        def _():
            pl.semaphore_signal(barrier, inc=1, device_id=holder(h, part), device_id_type=MESH)

    for d in range(1, parts):
        pl.semaphore_signal(
            barrier, inc=1, device_id=holder(me, lax.rem(part + d, parts)), device_id_type=MESH
        )

    padded = ids_out.shape[1]
    above = lax.broadcasted_iota(jnp.int32, (rows, padded), 0)
    across = lax.broadcasted_iota(jnp.int32, (rows, padded), 1)
    lab = jnp.sum(jnp.where(above == across, lcol_ref[...] + 1, 0), axis=0, keepdims=True) - 1
    earlier = (lcol_ref[...] == lab) & (above < across)
    rank = jnp.sum(earlier.astype(jnp.int32), axis=0, keepdims=True)
    target = jnp.where(lab >= 0, lab * cap + rank, -1)
    ids_out[...] = target
    ids_all[part, me] = target
    unit = (lax.broadcasted_iota(jnp.int32, (GROUP * cap, size), 1) == 0).astype(jnp.bfloat16)
    for c in range(groups):
        q_slots[c, :, size:] = unit

    pl.semaphore_wait(barrier, HEADS - 1 + parts - 1)

    def id_copy(h):
        return pltpu.make_async_remote_copy(
            ids_out, ids_all.at[part, me], id_ss.at[h], id_rs.at[me],
            device_id=holder(h, part), device_id_type=MESH)

    def kv_copy(h):
        return pltpu.make_async_remote_copy(
            kv_out.at[h], kv_all.at[part, me], kv_ss.at[h], kv_rs.at[me],
            device_id=holder(h, part), device_id_type=MESH)

    def q_copy(h):
        return pltpu.make_async_remote_copy(
            q_out.at[h], q_in.at[me], q_ss.at[h], q_rs.at[me],
            device_id=holder(h, part), device_id_type=MESH)

    def ret_copy(s):
        return pltpu.make_async_remote_copy(
            ret_out.at[s], gathered.at[:, pl.ds(pl.multiple_of(me * size, size), size)],
            ret_ss.at[s], ret_rs.at[me], device_id=holder(s, part), device_id_type=MESH)

    def kv_fwd(s, d):
        return pltpu.make_async_remote_copy(
            kv_all.at[part, s], kv_all.at[part, s], fkv_ss.at[d - 1, s], fkv_rs.at[d - 1, s],
            device_id=holder(me, lax.rem(part + d, parts)), device_id_type=MESH)

    def id_fwd(s, d):
        return pltpu.make_async_remote_copy(
            ids_all.at[part, s], ids_all.at[part, s], fid_ss.at[d - 1, s], fid_rs.at[d - 1, s],
            device_id=holder(me, lax.rem(part + d, parts)), device_id_type=MESH)

    @pl.loop(0, HEADS)
    def _(h):
        @pl.when(h != me)
        def _():
            id_copy(h).start()

    @pl.loop(0, pairs)
    def _(t):
        slot = lax.rem(t, 2)

        @pl.when(t + 1 < pairs)
        def _():
            for copy in w_copies(t + 1, 1 - slot):
                copy.start()

        for copy in w_copies(t, slot):
            copy.wait()
        made = jnp.dot(tok_ref[...], w_buf[slot], preferred_element_type=jnp.float32).astype(jnp.bfloat16)
        for j in range(PAIR):
            h = pair_out(t) * PAIR + j
            q = made[:, j * size:(j + 1) * size]
            k = made[:, pw + j * size:pw + (j + 1) * size]
            v = made[:, 2 * pw + j * size:2 * pw + (j + 1) * size]

            @pl.when(h != me)
            def _():
                kv_out[h, :, :size] = k
                kv_out[h, :, size:] = v
                q_out[h] = q
                kv_copy(h).start()

            @pl.when(h == me)
            def _():
                kv_all[part, me, :, :size] = k
                kv_all[part, me, :, size:] = v
                q_in[me] = q

    @pl.loop(0, HEADS)
    def _(i):
        h = lax.rem(own_pair * PAIR + i, HEADS)

        @pl.when(h != me)
        def _():
            q_copy(h).start()

    def spread(its_part, s):
        where = ids_all[its_part, s][:, :rows]
        return lax.broadcasted_iota(jnp.int32, (slots, rows), 0) == where

    def place_kv(its_part, s):
        hot = spread(its_part, s)
        placed = jnp.dot(
            hot.astype(jnp.bfloat16), kv_all[its_part, s], preferred_element_type=jnp.float32
        ).astype(jnp.bfloat16)
        live = jnp.sum(hot.astype(jnp.float32), axis=1, keepdims=True)
        bias = jnp.broadcast_to(jnp.where(live > 0, 0.0, MASKED_SCORE), (slots, size)).astype(jnp.bfloat16)
        at = pl.ds(pl.multiple_of((its_part * HEADS + s) * cap, cap), cap)
        for c in range(groups):
            mine = slice(c * cap, (c + 1) * cap)
            k_slots[c, at, :size] = placed[mine, :size]
            k_slots[c, at, size:] = bias[mine]
            v_slots[c, at, :] = placed[mine, size:]

    @pl.loop(0, HEADS)
    def _(i):
        s = source_at(i)

        @pl.when(s != me)
        def _():
            pltpu.make_async_remote_copy(
                ids_out, ids_all.at[part, s], id_ss.at[s], id_rs.at[s],
                device_id=holder(s, part), device_id_type=MESH).wait_recv()
            pltpu.make_async_remote_copy(
                kv_out.at[s], kv_all.at[part, s], kv_ss.at[s], kv_rs.at[s],
                device_id=holder(s, part), device_id_type=MESH).wait_recv()

        for d in range(1, parts):
            id_fwd(s, d).start()
            kv_fwd(s, d).start()
        place_kv(part, s)

    for d in range(1, parts):
        frm = lax.rem(part + parts - d, parts)

        @pl.loop(0, HEADS)
        def _(i):
            s = source_at(i)
            pltpu.make_async_remote_copy(
                ids_all.at[frm, s], ids_all.at[frm, s], fid_ss.at[d - 1, s], fid_rs.at[d - 1, s],
                device_id=holder(me, frm), device_id_type=MESH).wait_recv()
            pltpu.make_async_remote_copy(
                kv_all.at[frm, s], kv_all.at[frm, s], fkv_ss.at[d - 1, s], fkv_rs.at[d - 1, s],
                device_id=holder(me, frm), device_id_type=MESH).wait_recv()
            place_kv(frm, s)

    factor = LOG2E * size ** (-0.5)

    @pl.loop(0, HEADS // GROUP)
    def _(g):
        for n in range(GROUP):
            s = source_at(g * GROUP + n)

            @pl.when(s != me)
            def _():
                pltpu.make_async_remote_copy(
                    q_out.at[s], q_in.at[s], q_ss.at[s], q_rs.at[s],
                    device_id=holder(s, part), device_id_type=MESH).wait_recv()

            placed = jnp.dot(
                spread(part, s).astype(jnp.bfloat16), q_in[s], preferred_element_type=jnp.float32
            ).astype(jnp.bfloat16)
            for c in range(groups):
                q_slots[c, n * cap:(n + 1) * cap, :size] = placed[c * cap:(c + 1) * cap]

        def attend(c):
            scores = lax.dot_general(
                q_slots[c], k_slots[c], (((1,), (1,)), ((), ())), preferred_element_type=jnp.float32
            )
            top = jnp.max(scores, axis=1, keepdims=True)
            weights = jnp.exp2((scores - top) * factor)
            total = jnp.sum(weights, axis=1, keepdims=True)
            summed = jnp.dot(
                weights.astype(jnp.bfloat16), v_slots[c], preferred_element_type=jnp.float32
            )
            att_slots[c] = (summed / total).astype(jnp.bfloat16)

        if groups <= 4:
            for c in range(groups):
                attend(c)
        else:
            pl.loop(0, groups)(attend)

        for n in range(GROUP):
            s = source_at(g * GROUP + n)
            mine = jnp.concatenate(
                [att_slots[c, n * cap:(n + 1) * cap, :] for c in range(groups)], axis=0
            )
            back = lax.dot_general(
                spread(part, s).astype(jnp.bfloat16), mine, (((0,), (0,)), ((), ())),
                preferred_element_type=jnp.float32,
            ).astype(jnp.bfloat16)
            ret_out[s] = back

            @pl.when(s != me)
            def _():
                ret_copy(s).start()

            @pl.when(s == me)
            def _():
                own = pltpu.make_async_copy(
                    ret_out.at[s], gathered.at[:, pl.ds(pl.multiple_of(me * size, size), size)], own_sem)
                own.start()
                own.wait()

    @pl.loop(0, HEADS)
    def _(h):
        @pl.when(h != me)
        def _():
            id_copy(h).wait_send()
            kv_copy(h).wait_send()
            q_copy(h).wait_send()
            ret_copy(h).wait_send()
            pltpu.make_async_remote_copy(
                ret_out.at[h], gathered.at[:, pl.ds(pl.multiple_of(h * size, size), size)],
                ret_ss.at[h], ret_rs.at[h], device_id=holder(h, part), device_id_type=MESH).wait_recv()

        for d in range(1, parts):
            id_fwd(h, d).wait_send()
            kv_fwd(h, d).wait_send()

    out_ref[...] = gathered[...]


def per_device(tokens, w_query, w_key, w_value, cluster_ids):
    groups, blks = lax.axis_size("cluster"), lax.axis_size("blk")
    rows, width = tokens.shape
    size = width // HEADS
    parts = groups * blks // HEADS
    cap = 4 * rows // (3 * groups)
    padded = -(-rows // 128) * 128
    vmem = pl.BlockSpec(memory_space=pltpu.VMEM)
    hbm = pl.BlockSpec(memory_space=pl.ANY)
    bf16 = jnp.bfloat16
    sem = pltpu.SemaphoreType.DMA
    others = max(parts - 1, 1)
    keys = parts * HEADS * cap
    return pl.pallas_call(
        functools.partial(kernel, groups, blks, parts, cap),
        out_shape=jax.ShapeDtypeStruct((rows, width), bf16),
        in_specs=[vmem, hbm, hbm, hbm, vmem],
        out_specs=vmem,
        scratch_shapes=[
            pltpu.VMEM((2, width, 3 * PAIR * size), bf16),
            pltpu.VMEM((HEADS, rows, 2 * size), bf16),
            pltpu.VMEM((HEADS, rows, size), bf16),
            pltpu.VMEM((1, padded), jnp.int32),
            pltpu.VMEM((parts, HEADS, rows, 2 * size), bf16),
            pltpu.VMEM((HEADS, rows, size), bf16),
            pltpu.VMEM((parts, HEADS, 1, padded), jnp.int32),
            pltpu.VMEM((groups, keys, 2 * size), bf16),
            pltpu.VMEM((groups, keys, size), bf16),
            pltpu.VMEM((groups, GROUP * cap, 2 * size), bf16),
            pltpu.VMEM((groups, GROUP * cap, size), bf16),
            pltpu.VMEM((HEADS, rows, size), bf16),
            pltpu.VMEM((rows, width), bf16),
            sem((2, 3)),
            sem((HEADS,)), sem((HEADS,)), sem((HEADS,)), sem((HEADS,)), sem((HEADS,)), sem((HEADS,)),
            sem((others, HEADS)), sem((others, HEADS)), sem((others, HEADS)), sem((others, HEADS)),
            sem((HEADS,)), sem((HEADS,)),
            sem,
        ],
        compiler_params=pltpu.CompilerParams(
            collective_id=0, has_side_effects=True, vmem_limit_bytes=60 * 1024 * 1024
        ),
    )(tokens, w_query, w_key, w_value, cluster_ids)


def solution(mesh):
    return jax.shard_map(
        per_device,
        mesh=mesh,
        in_specs=(P(("cluster", "blk"), None), P(), P(), P(), P(("cluster", "blk"), None)),
        out_specs=P(("cluster", "blk"), None),
        check_vma=False,
    )
```

```python
import functools

import jax
import jax.numpy as jnp
from jax import lax
from jax.experimental import pallas as pl
from jax.experimental.pallas import tpu as pltpu
from jax.sharding import PartitionSpec as P

HEADS = 16
MASKED_SCORE = -1e30
LOG2E = 1.4426950408889634
PAIR = 2
GROUP = 4
MESH = pl.DeviceIdType.MESH


def kernel(groups, blks, parts, cap, tok_ref, wq_ref, wk_ref, wv_ref, lcol_ref, out_ref,
           w_buf, kv_out, q_out, ids_out, kv_all, q_in, ids_all, k_slots, v_slots, q_slots, att_slots,
           ret_out, gathered, w_sem, kv_ss, kv_rs, q_ss, q_rs, id_ss, id_rs, fkv_ss, fkv_rs, fid_ss,
           fid_rs, ret_ss, ret_rs, own_sem):
    rows, width = tok_ref.shape
    size = width // HEADS
    slots = groups * cap
    pairs = HEADS // PAIR
    pw = PAIR * size
    ci, bi = lax.axis_index("cluster"), lax.axis_index("blk")
    part = lax.rem(ci, parts)
    me = (ci // parts) * blks + bi
    own_pair = me // PAIR

    def holder(head, its_part):
        return {"cluster": (head // blks) * parts + its_part, "blk": lax.rem(head, blks)}

    def pair_out(t):
        return lax.rem(own_pair + t, pairs)

    def source_at(i):
        return lax.rem(own_pair + pairs - i // PAIR, pairs) * PAIR + lax.rem(i, PAIR)

    def w_copies(t, slot):
        cols = pl.ds(pl.multiple_of(pair_out(t) * pw, pw), pw)
        return [
            pltpu.make_async_copy(ref.at[:, cols], w_buf.at[slot, :, pl.ds(n * pw, pw)], w_sem.at[slot, n])
            for n, ref in enumerate((wq_ref, wk_ref, wv_ref))
        ]

    for t in range(2):
        for copy in w_copies(t, t):
            copy.start()

    barrier = pltpu.get_barrier_semaphore()

    @pl.loop(0, HEADS)
    def _(h):
        @pl.when(h != me)
        def _():
            pl.semaphore_signal(barrier, inc=1, device_id=holder(h, part), device_id_type=MESH)

    for d in range(1, parts):
        pl.semaphore_signal(
            barrier, inc=1, device_id=holder(me, lax.rem(part + d, parts)), device_id_type=MESH
        )

    padded = ids_out.shape[1]
    above = lax.broadcasted_iota(jnp.int32, (rows, padded), 0)
    across = lax.broadcasted_iota(jnp.int32, (rows, padded), 1)
    lab = jnp.sum(jnp.where(above == across, lcol_ref[...] + 1, 0), axis=0, keepdims=True) - 1
    earlier = (lcol_ref[...] == lab) & (above < across)
    rank = jnp.sum(earlier.astype(jnp.int32), axis=0, keepdims=True)
    target = jnp.where(lab >= 0, lab * cap + rank, -1)
    ids_out[...] = target
    ids_all[part, me] = target
    unit = (lax.broadcasted_iota(jnp.int32, (GROUP * cap, size), 1) == 0).astype(jnp.bfloat16)
    for c in range(groups):
        q_slots[c, :, size:] = unit

    pl.semaphore_wait(barrier, HEADS - 1 + parts - 1)

    def id_copy(h):
        return pltpu.make_async_remote_copy(
            ids_out, ids_all.at[part, me], id_ss.at[h], id_rs.at[me],
            device_id=holder(h, part), device_id_type=MESH)

    def kv_copy(h):
        return pltpu.make_async_remote_copy(
            kv_out.at[h], kv_all.at[part, me], kv_ss.at[h], kv_rs.at[me],
            device_id=holder(h, part), device_id_type=MESH)

    def q_copy(h):
        return pltpu.make_async_remote_copy(
            q_out.at[h], q_in.at[me], q_ss.at[h], q_rs.at[me],
            device_id=holder(h, part), device_id_type=MESH)

    def ret_copy(s):
        return pltpu.make_async_remote_copy(
            ret_out.at[s], gathered.at[:, pl.ds(pl.multiple_of(me * size, size), size)],
            ret_ss.at[s], ret_rs.at[me], device_id=holder(s, part), device_id_type=MESH)

    def kv_fwd(s, d):
        return pltpu.make_async_remote_copy(
            kv_all.at[part, s], kv_all.at[part, s], fkv_ss.at[d - 1, s], fkv_rs.at[d - 1, s],
            device_id=holder(me, lax.rem(part + d, parts)), device_id_type=MESH)

    def id_fwd(s, d):
        return pltpu.make_async_remote_copy(
            ids_all.at[part, s], ids_all.at[part, s], fid_ss.at[d - 1, s], fid_rs.at[d - 1, s],
            device_id=holder(me, lax.rem(part + d, parts)), device_id_type=MESH)

    @pl.loop(0, HEADS)
    def _(h):
        @pl.when(h != me)
        def _():
            id_copy(h).start()

    @pl.loop(0, pairs)
    def _(t):
        slot = lax.rem(t, 3)

        @pl.when(t + 2 < pairs)
        def _():
            for copy in w_copies(t + 2, lax.rem(t + 2, 3)):
                copy.start()

        for copy in w_copies(t, slot):
            copy.wait()
        made = jnp.dot(tok_ref[...], w_buf[slot], preferred_element_type=jnp.float32).astype(jnp.bfloat16)
        for j in range(PAIR):
            h = pair_out(t) * PAIR + j
            q = made[:, j * size:(j + 1) * size]
            k = made[:, pw + j * size:pw + (j + 1) * size]
            v = made[:, 2 * pw + j * size:2 * pw + (j + 1) * size]

            @pl.when(h != me)
            def _():
                kv_out[h, :, :size] = k
                kv_out[h, :, size:] = v
                q_out[h] = q
                kv_copy(h).start()

            @pl.when(h == me)
            def _():
                kv_all[part, me, :, :size] = k
                kv_all[part, me, :, size:] = v
                q_in[me] = q

    @pl.loop(0, HEADS)
    def _(i):
        h = lax.rem(own_pair * PAIR + i, HEADS)

        @pl.when(h != me)
        def _():
            q_copy(h).start()

    def spread(its_part, s):
        where = ids_all[its_part, s][:, :rows]
        return lax.broadcasted_iota(jnp.int32, (slots, rows), 0) == where

    def place_kv(its_part, s):
        hot = spread(its_part, s)
        placed = jnp.dot(
            hot.astype(jnp.bfloat16), kv_all[its_part, s], preferred_element_type=jnp.float32
        ).astype(jnp.bfloat16)
        live = jnp.sum(hot.astype(jnp.float32), axis=1, keepdims=True)
        bias = jnp.broadcast_to(jnp.where(live > 0, 0.0, MASKED_SCORE), (slots, size)).astype(jnp.bfloat16)
        at = pl.ds(pl.multiple_of((its_part * HEADS + s) * cap, cap), cap)
        for c in range(groups):
            mine = slice(c * cap, (c + 1) * cap)
            k_slots[c, at, :size] = placed[mine, :size]
            k_slots[c, at, size:] = bias[mine]
            v_slots[c, at, :] = placed[mine, size:]

    @pl.loop(0, HEADS)
    def _(i):
        s = source_at(i)

        @pl.when(s != me)
        def _():
            pltpu.make_async_remote_copy(
                ids_out, ids_all.at[part, s], id_ss.at[s], id_rs.at[s],
                device_id=holder(s, part), device_id_type=MESH).wait_recv()
            pltpu.make_async_remote_copy(
                kv_out.at[s], kv_all.at[part, s], kv_ss.at[s], kv_rs.at[s],
                device_id=holder(s, part), device_id_type=MESH).wait_recv()

        for d in range(1, parts):
            id_fwd(s, d).start()
            kv_fwd(s, d).start()
        place_kv(part, s)

    for d in range(1, parts):
        frm = lax.rem(part + parts - d, parts)

        @pl.loop(0, HEADS)
        def _(i):
            s = source_at(i)
            pltpu.make_async_remote_copy(
                ids_all.at[frm, s], ids_all.at[frm, s], fid_ss.at[d - 1, s], fid_rs.at[d - 1, s],
                device_id=holder(me, frm), device_id_type=MESH).wait_recv()
            pltpu.make_async_remote_copy(
                kv_all.at[frm, s], kv_all.at[frm, s], fkv_ss.at[d - 1, s], fkv_rs.at[d - 1, s],
                device_id=holder(me, frm), device_id_type=MESH).wait_recv()
            place_kv(frm, s)

    factor = LOG2E * size ** (-0.5)

    @pl.loop(0, HEADS // GROUP)
    def _(g):
        for n in range(GROUP):
            s = source_at(g * GROUP + n)

            @pl.when(s != me)
            def _():
                pltpu.make_async_remote_copy(
                    q_out.at[s], q_in.at[s], q_ss.at[s], q_rs.at[s],
                    device_id=holder(s, part), device_id_type=MESH).wait_recv()

            placed = jnp.dot(
                spread(part, s).astype(jnp.bfloat16), q_in[s], preferred_element_type=jnp.float32
            ).astype(jnp.bfloat16)
            for c in range(groups):
                q_slots[c, n * cap:(n + 1) * cap, :size] = placed[c * cap:(c + 1) * cap]

        def attend(c):
            scores = lax.dot_general(
                q_slots[c], k_slots[c], (((1,), (1,)), ((), ())), preferred_element_type=jnp.float32
            )
            top = jnp.max(scores, axis=1, keepdims=True)
            weights = jnp.exp2((scores - top) * factor)
            total = jnp.sum(weights, axis=1, keepdims=True)
            summed = jnp.dot(
                weights.astype(jnp.bfloat16), v_slots[c], preferred_element_type=jnp.float32
            )
            att_slots[c] = (summed / total).astype(jnp.bfloat16)

        if groups <= 4:
            for c in range(groups):
                attend(c)
        else:
            pl.loop(0, groups)(attend)

        for n in range(GROUP):
            s = source_at(g * GROUP + n)
            mine = jnp.concatenate(
                [att_slots[c, n * cap:(n + 1) * cap, :] for c in range(groups)], axis=0
            )
            back = lax.dot_general(
                spread(part, s).astype(jnp.bfloat16), mine, (((0,), (0,)), ((), ())),
                preferred_element_type=jnp.float32,
            ).astype(jnp.bfloat16)
            ret_out[s] = back

            @pl.when(s != me)
            def _():
                ret_copy(s).start()

            @pl.when(s == me)
            def _():
                own = pltpu.make_async_copy(
                    ret_out.at[s], gathered.at[:, pl.ds(pl.multiple_of(me * size, size), size)], own_sem)
                own.start()
                own.wait()

    @pl.loop(0, HEADS)
    def _(h):
        @pl.when(h != me)
        def _():
            id_copy(h).wait_send()
            kv_copy(h).wait_send()
            q_copy(h).wait_send()
            ret_copy(h).wait_send()
            pltpu.make_async_remote_copy(
                ret_out.at[h], gathered.at[:, pl.ds(pl.multiple_of(h * size, size), size)],
                ret_ss.at[h], ret_rs.at[h], device_id=holder(h, part), device_id_type=MESH).wait_recv()

        for d in range(1, parts):
            id_fwd(h, d).wait_send()
            kv_fwd(h, d).wait_send()

    out_ref[...] = gathered[...]


def per_device(tokens, w_query, w_key, w_value, cluster_ids):
    groups, blks = lax.axis_size("cluster"), lax.axis_size("blk")
    rows, width = tokens.shape
    size = width // HEADS
    parts = groups * blks // HEADS
    cap = 4 * rows // (3 * groups)
    padded = -(-rows // 128) * 128
    vmem = pl.BlockSpec(memory_space=pltpu.VMEM)
    hbm = pl.BlockSpec(memory_space=pl.ANY)
    bf16 = jnp.bfloat16
    sem = pltpu.SemaphoreType.DMA
    others = max(parts - 1, 1)
    keys = parts * HEADS * cap
    return pl.pallas_call(
        functools.partial(kernel, groups, blks, parts, cap),
        out_shape=jax.ShapeDtypeStruct((rows, width), bf16),
        in_specs=[vmem, hbm, hbm, hbm, vmem],
        out_specs=vmem,
        scratch_shapes=[
            pltpu.VMEM((3, width, 3 * PAIR * size), bf16),
            pltpu.VMEM((HEADS, rows, 2 * size), bf16),
            pltpu.VMEM((HEADS, rows, size), bf16),
            pltpu.VMEM((1, padded), jnp.int32),
            pltpu.VMEM((parts, HEADS, rows, 2 * size), bf16),
            pltpu.VMEM((HEADS, rows, size), bf16),
            pltpu.VMEM((parts, HEADS, 1, padded), jnp.int32),
            pltpu.VMEM((groups, keys, 2 * size), bf16),
            pltpu.VMEM((groups, keys, size), bf16),
            pltpu.VMEM((groups, GROUP * cap, 2 * size), bf16),
            pltpu.VMEM((groups, GROUP * cap, size), bf16),
            pltpu.VMEM((HEADS, rows, size), bf16),
            pltpu.VMEM((rows, width), bf16),
            sem((3, 3)),
            sem((HEADS,)), sem((HEADS,)), sem((HEADS,)), sem((HEADS,)), sem((HEADS,)), sem((HEADS,)),
            sem((others, HEADS)), sem((others, HEADS)), sem((others, HEADS)), sem((others, HEADS)),
            sem((HEADS,)), sem((HEADS,)),
            sem,
        ],
        compiler_params=pltpu.CompilerParams(
            collective_id=0, has_side_effects=True, vmem_limit_bytes=62 * 1024 * 1024
        ),
    )(tokens, w_query, w_key, w_value, cluster_ids)


def solution(mesh):
    return jax.shard_map(
        per_device,
        mesh=mesh,
        in_specs=(P(("cluster", "blk"), None), P(), P(), P(), P(("cluster", "blk"), None)),
        out_specs=P(("cluster", "blk"), None),
        check_vma=False,
    )
```
